32 devices in a mesh: area: 16 (over z, y, core), win: 2 (over x).
Axes of the slice: x: 2, y: 2, z: 4, core: 2. Of those that a mesh axis runs over, the one named last changes fastest.
Arguments:
- kkt: bfloat16 [16, 2, 1536, 1536], P('area', 'win'), as said below
- offsets: float32 [16, 2, 1536, 256], P('area', 'win'), may hold values from -6 to 6
- lower: float32 [16, 2, 1536], P('area', 'win'), may hold values from -1.2 to -0.4
- upper: float32 [16, 2, 1536], P('area', 'win'), may hold values from 0.4 to 1.2
- partners: int32 [4, 16], replicated, may hold values from 0 to 15, as said below
- adjacency: int32 [16, 16], replicated, may hold values from 0 to 1, as said below
Outputs:
- consensus: float32 [16, 2, 1536, 256], P('area', 'win')
- duals: float32 [16, 2, 1536, 256], P('area', 'win')
The draws below stay inside these ranges and needn't reach their ends.
Inputs may be any that keep to these rules, and one draw needn't show every extreme that they name: `partners`: row k is the perfect matching a -> a XOR c_k for a colour c_k between 1 and 15. `adjacency`: symmetric with a zero diagonal. `kkt`: each block is a dense full-rank matrix with a positive diagonal.
All inputs are finite; a program needn't handle non-finite values.
Results may differ from the reference program's by a relative error of at most 0.0028.
Values sent between devices are 32-bit elements; how exact they have to be, the bound alone decides.
A program may use at most 64 MiB of HBM per device.

```python
import jax
import jax.numpy as jnp
from jax import lax

K = 1536
COUPLE = 512
BOUND = 256
S = 256
ITERS = 4
N_AREA = 16
N_WIN = 2


def draw_kkt(key, part):
    key_off = jax.random.fold_in(key, 11)
    key_diag = jax.random.fold_in(key, 12)
    off = jax.random.normal(key_off, (N_AREA, N_WIN, K, K), jnp.float32) * 0.4 / jnp.sqrt(1.0 * K)
    diag = jnp.exp(jax.random.uniform(key_diag, (N_AREA, N_WIN, K, 1), jnp.float32, jnp.log(0.4), jnp.log(1.2)))
    eye = jnp.eye(K, dtype=jnp.float32)
    return (off + eye[None, None] * diag).astype(jnp.bfloat16)


def draw_partners(key, part):
    colours = jax.random.randint(jax.random.fold_in(key, 21), (ITERS,), 1, N_AREA)
    areas = jnp.arange(N_AREA, dtype=jnp.int32)
    return jnp.bitwise_xor(areas[None, :], colours[:, None]).astype(jnp.int32)


def draw_adjacency(key, part):
    bits = jax.random.randint(jax.random.fold_in(key, 31), (N_AREA, N_AREA), 0, 2)
    upper_part = jnp.triu(bits, 1)
    return (upper_part + upper_part.T).astype(jnp.int32)


def steps_of(own_key, extent, cuts, least, top_value):
    level, own = 1.0, jax.random.fold_in(own_key, 6)
    for axis_at, parts in cuts:
        heights = jnp.exp(jax.random.uniform(jax.random.fold_in(own, axis_at), (parts,), jnp.float32, least / len(cuts), top_value / len(cuts)))
        level = level * jnp.repeat(heights, extent[axis_at] // parts).reshape([-1 if axis == axis_at else 1 for axis in range(len(extent))])
    return level


def normal_values(rng, dims, scale, limit, split=(), kind=jnp.bfloat16):
    entries = jax.random.normal(rng, dims, jnp.float32) * scale
    if len(split) > 0:
        entries = steps_of(rng, dims, split, -0.22, 0.18) * entries
    return jnp.clip(entries, min=-limit, max=limit).astype(kind)


def setup_inputs(seed: int = 0) -> dict:
    streams_of = jax.random.split(jax.random.key(seed), 7)
    return {
        "kkt": draw_kkt(jax.random.fold_in(streams_of[6], 71), 0),
        "offsets": normal_values(streams_of[1], (N_AREA, N_WIN, K, S), 1.0, 6.0, ((0, 16), (1, 2)), jnp.float32),
        "lower": jnp.clip(-1.2 + 0.800000042 * jax.random.uniform(streams_of[2], (N_AREA, N_WIN, K), jnp.float32) ** steps_of(streams_of[2], (N_AREA, N_WIN, K), ((0, 16), (1, 2)), -0.2, 0.2), -1.2, -0.4),
        "upper": jnp.clip(0.4 + 0.800000042 * jax.random.uniform(streams_of[3], (N_AREA, N_WIN, K), jnp.float32) ** steps_of(streams_of[3], (N_AREA, N_WIN, K), ((0, 16), (1, 2)), -0.2, 0.2), 0.4, 1.2),
        "partners": draw_partners(jax.random.fold_in(streams_of[6], 71), 0),
        "adjacency": draw_adjacency(jax.random.fold_in(streams_of[6], 71), 0),
    }


def apply_block(pair):
    return jnp.dot(pair[0], pair[1], preferred_element_type=jnp.float32)


def reference(kkt, offsets, lower, upper, partners, adjacency):
    z_now = jnp.zeros_like(offsets)
    u_now = jnp.zeros_like(offsets)
    low = lower[..., None]
    high = upper[..., None]
    areas = jnp.arange(N_AREA).astype(jnp.int32)
    flat_kkt = kkt.reshape(N_AREA * N_WIN, K, K)
    for step in range(ITERS):
        v_now = (offsets + z_now - u_now).astype(jnp.bfloat16)
        x_now = lax.map(apply_block, (flat_kkt, v_now.reshape(N_AREA * N_WIN, K, S)))
        x_now = x_now.reshape(N_AREA, N_WIN, K, S)
        y_now = jnp.minimum(jnp.maximum(x_now + u_now, low), high)
        row = partners[step]
        couple = y_now[:, :, :COUPLE]
        other = couple[row]
        linked = (adjacency[areas, row] == 1).astype(offsets.dtype)[:, None, None, None]
        new_couple = couple + linked * 0.5 * (other - couple)
        ends = y_now[:, :, COUPLE:COUPLE + BOUND]
        before = jnp.concatenate([jnp.zeros_like(ends[:, :1]), ends[:, :-1]], axis=1)
        starts = 0.5 * (y_now[:, :, COUPLE + BOUND:COUPLE + 2 * BOUND] + before)
        z_now = jnp.concatenate([new_couple, ends, starts, y_now[:, :, COUPLE + 2 * BOUND:]], axis=2)
        u_now = u_now + x_now - z_now
    return z_now, u_now
```

```python
import functools

import jax
import jax.numpy as jnp
from jax import lax
from jax.experimental import pallas as pl
from jax.experimental.pallas import tpu as pltpu
from jax.sharding import PartitionSpec as P

COUPLE = 512
BOUND = 256
ITERS = 4
TILE = 256
MESH = pl.DeviceIdType.MESH


def mate_of(area, colour):
    mate = area
    bit = 1
    while bit <= colour:
        if colour & bit:
            mate = mate + bit - 2 * bit * lax.rem(lax.div(area, bit), 2)
        bit *= 2
    return mate


def iteration(colour, windows, half_link, kkt, costs, bounds, u_in, v_in, u_out, v_out, z_out,
              kk, vv, cc, bb, tt, yy, got, before, load, store, load_v, send, recv):
    size = kk.shape[0]
    tiles = size // TILE
    coupled = COUPLE // TILE
    end_tile = coupled
    start_tile = coupled + BOUND // TILE
    area = lax.axis_index("area")
    win = lax.axis_index("win")
    mate = mate_of(area, colour)

    def rows(i):
        return pl.ds(i * TILE, TILE)

    def loading(which, source, target, i):
        return pltpu.make_async_copy(source.at[rows(i)], target.at[rows(i)], load.at[which, i])

    def storing(which, source, target, i):
        return pltpu.make_async_copy(source.at[rows(i)], target.at[rows(i)], store.at[which, i])

    whole_v = pltpu.make_async_copy(v_in, vv, load_v)
    whole_v.start()
    for i in range(tiles):
        loading(0, kkt, kk, i).start()
        loading(1, u_in, tt, i).start()
        loading(2, bounds, bb, i).start()

    barrier = pltpu.get_barrier_semaphore()
    pl.semaphore_signal(barrier, inc=1, device_id=(mate, win), device_id_type=MESH)

    @pl.when(win > 0)
    def _():
        pl.semaphore_signal(barrier, inc=1, device_id=(area, win - 1), device_id_type=MESH)

    @pl.when(win == 0)
    def _():
        before[...] = jnp.zeros_like(before)

    for i in range(tiles):
        loading(3, costs, cc, i).start()

    def to_mate(i):
        return pltpu.make_async_remote_copy(
            src_ref=yy.at[rows(i)], dst_ref=got.at[rows(i)], send_sem=send.at[i], recv_sem=recv.at[i],
            device_id=(mate, win), device_id_type=MESH)

    ends = pltpu.make_async_remote_copy(
        src_ref=yy.at[rows(end_tile)], dst_ref=before, send_sem=send.at[coupled], recv_sem=recv.at[coupled],
        device_id=(area, win + 1), device_id_type=MESH)

    whole_v.wait()
    for i in range(tiles):
        for which, source, target in ((0, kkt, kk), (1, u_in, tt), (2, bounds, bb)):
            loading(which, source, target, i).wait()
        x = jnp.dot(kk[rows(i), :], vv[...], preferred_element_type=jnp.float32)
        t = x + tt[rows(i), :]
        tt[rows(i), :] = t
        yy[rows(i), :] = jnp.minimum(jnp.maximum(t, bb[rows(i), 0:1]), bb[rows(i), 1:2])
        if i == 0:
            @pl.when(win < windows - 1)
            def _():
                pl.semaphore_wait(barrier, 2)

            @pl.when(win == windows - 1)
            def _():
                pl.semaphore_wait(barrier, 1)

        if i < coupled:
            to_mate(i).start()
        if i == end_tile:
            @pl.when(win < windows - 1)
            def _():
                ends.start()

    def finish(i, z, source):
        u = tt[rows(i), :] - z
        tt[rows(i), :] = u
        loading(3, costs, cc, i).wait()
        vv[rows(i), :] = (cc[rows(i), :] + z - u).astype(jnp.bfloat16)
        storing(0, tt, u_out, i).start()
        storing(1, vv, v_out, i).start()
        storing(2, source, z_out, i).start()

    for i in range(coupled, tiles):
        if i != start_tile:
            finish(i, yy[rows(i), :], yy)

    @pl.when(win > 0)
    def _():
        ends.wait_recv()

    z = 0.5 * (yy[rows(start_tile), :] + before[...])
    yy[rows(start_tile), :] = z
    finish(start_tile, z, yy)

    for i in range(coupled):
        to_mate(i).wait_recv()
        y = yy[rows(i), :]
        z = y + half_link[0] * (got[rows(i), :] - y)
        got[rows(i), :] = z
        finish(i, z, got)

    for i in range(coupled):
        to_mate(i).wait_send()

    @pl.when(win < windows - 1)
    def _():
        ends.wait_send()

    for i in range(tiles):
        storing(0, tt, u_out, i).wait()
        storing(1, vv, v_out, i).wait()
        storing(2, got if i < coupled else yy, z_out, i).wait()


def run_colour(half_link, kkt, costs, bounds, u, v, *, colour, windows):
    size, columns = costs.shape
    tiles = size // TILE
    coupled = COUPLE // TILE
    anywhere = pl.BlockSpec(memory_space=pl.ANY)
    return pl.pallas_call(
        functools.partial(iteration, colour, windows),
        out_shape=(
            jax.ShapeDtypeStruct(u.shape, u.dtype),
            jax.ShapeDtypeStruct(v.shape, v.dtype),
            jax.ShapeDtypeStruct(u.shape, u.dtype),
        ),
        in_specs=[pl.BlockSpec(memory_space=pltpu.SMEM)] + [anywhere] * 5,
        out_specs=(anywhere,) * 3,
        scratch_shapes=[
            pltpu.VMEM((size, size), jnp.bfloat16),
            pltpu.VMEM((size, columns), jnp.bfloat16),
            pltpu.VMEM((size, columns), jnp.float32),
            pltpu.VMEM((size, 2), jnp.float32),
            pltpu.VMEM((size, columns), jnp.float32),
            pltpu.VMEM((size, columns), jnp.float32),
            pltpu.VMEM((COUPLE, columns), jnp.float32),
            pltpu.VMEM((BOUND, columns), jnp.float32),
            pltpu.SemaphoreType.DMA((4, tiles)),
            pltpu.SemaphoreType.DMA((3, tiles)),
            pltpu.SemaphoreType.DMA,
            pltpu.SemaphoreType.DMA((coupled + 1,)),
            pltpu.SemaphoreType.DMA((coupled + 1,)),
        ],
        compiler_params=pltpu.CompilerParams(
            collective_id=colour, has_side_effects=True, vmem_limit_bytes=32 * 1024 * 1024),
        name="iteration_%d" % colour,
    )(half_link, kkt, costs, bounds, u, v)


def local(kkt, offsets, lower, upper, partners, adjacency):
    matrix = kkt[0, 0]
    costs = offsets[0, 0]
    bounds = jnp.stack([lower[0, 0], upper[0, 0]], axis=1)
    area = lax.axis_index("area")
    count = lax.axis_size("area")
    windows = lax.axis_size("win")
    colours = partners[:, 0]
    mates = lax.dynamic_index_in_dim(partners, area, 1, keepdims=False)
    linked = adjacency[area][mates] == 1
    half_links = 0.5 * linked.astype(costs.dtype)
    branches = [functools.partial(run_colour, colour=c, windows=windows) for c in range(1, count)]

    def step(k, state):
        u, v, _ = state
        half_link = lax.dynamic_slice_in_dim(half_links, k, 1)
        return lax.switch(colours[k] - 1, branches, half_link, matrix, costs, bounds, u, v)

    start = jnp.zeros_like(costs)
    u, _, z = lax.fori_loop(0, ITERS, step, (start, costs.astype(jnp.bfloat16), start))
    return (z[None, None], u[None, None])


def solution(mesh):
    in_specs = (
        P("area", "win", None, None),
        P("area", "win", None, None),
        P("area", "win", None),
        P("area", "win", None),
        P(),
        P(),
    )
    out_specs = (P("area", "win", None, None), P("area", "win", None, None))
    return jax.shard_map(local, mesh=mesh, in_specs=in_specs, out_specs=out_specs, check_vma=False)
```

```python
import functools

import jax
import jax.numpy as jnp
from jax import lax
from jax.experimental import pallas as pl
from jax.experimental.pallas import tpu as pltpu
from jax.sharding import PartitionSpec as P

COUPLE = 512
BOUND = 256
ITERS = 4
TILE = 256
PART = 128
MESH = pl.DeviceIdType.MESH


def mate_of(area, colour):
    mate = area
    bit = 1
    while bit <= colour:
        if colour & bit:
            mate = mate + bit - 2 * bit * lax.rem(lax.div(area, bit), 2)
        bit *= 2
    return mate


def exchange(colour, windows, y, got, before, send, recv):
    area = lax.axis_index("area")
    win = lax.axis_index("win")
    mate = mate_of(area, colour)
    barrier = pltpu.get_barrier_semaphore()
    pl.semaphore_signal(barrier, inc=1, device_id=(mate, win), device_id_type=MESH)

    @pl.when(win > 0)
    def _():
        pl.semaphore_signal(barrier, inc=1, device_id=(area, win - 1), device_id_type=MESH)

    @pl.when(win < windows - 1)
    def _():
        pl.semaphore_wait(barrier, 2)

    @pl.when(win == windows - 1)
    def _():
        pl.semaphore_wait(barrier, 1)

    couple = pltpu.make_async_remote_copy(
        src_ref=y.at[pl.ds(0, COUPLE)], dst_ref=got, send_sem=send.at[0], recv_sem=recv.at[0],
        device_id=(mate, win), device_id_type=MESH)
    ends = pltpu.make_async_remote_copy(
        src_ref=y.at[pl.ds(COUPLE, BOUND)], dst_ref=before, send_sem=send.at[1], recv_sem=recv.at[1],
        device_id=(area, win + 1), device_id_type=MESH)
    couple.start()

    @pl.when(win < windows - 1)
    def _():
        ends.start()

    @pl.when(win > 0)
    def _():
        ends.wait_recv()

    @pl.when(win < windows - 1)
    def _():
        ends.wait_send()

    couple.wait()


def run_exchange(y, *, colour, windows):
    columns = y.shape[1]
    anywhere = pl.BlockSpec(memory_space=pl.ANY)
    return pl.pallas_call(
        functools.partial(exchange, colour, windows),
        out_shape=(
            jax.ShapeDtypeStruct((COUPLE, columns), y.dtype),
            jax.ShapeDtypeStruct((BOUND, columns), y.dtype),
        ),
        in_specs=[anywhere],
        out_specs=(anywhere,) * 2,
        scratch_shapes=[pltpu.SemaphoreType.DMA((2,)), pltpu.SemaphoreType.DMA((2,))],
        compiler_params=pltpu.CompilerParams(
            collective_id=colour, has_side_effects=True, vmem_limit_bytes=1024 * 1024),
        name="exchange_%d" % colour,
    )(y)


def update(half_link, kkt, costs, bounds, t_in, got, before, t_out, y_out, v):
    win = lax.axis_index("win")
    size = kkt.shape[0]
    start_row = COUPLE + BOUND

    def clipped(rows, t):
        return jnp.minimum(jnp.maximum(t, bounds[rows, 0:1]), bounds[rows, 1:2])

    def settle(rows, t, z):
        u = t - z
        t_out[rows, :] = u
        v[rows, :] = (costs[rows, :] + z - u).astype(v.dtype)

    def coupled(i, _):
        rows = pl.ds(pl.multiple_of(i * PART, PART), PART)
        t = t_in[rows, :]
        y = clipped(rows, t)
        settle(rows, t, y + half_link[0] * (got[rows, :] - y))
        return _

    def starting(i, _):
        rows = pl.ds(pl.multiple_of(start_row + i * PART, PART), PART)
        t = t_in[rows, :]
        behind = jnp.where(win > 0, before[pl.ds(pl.multiple_of(i * PART, PART), PART), :], 0.0)
        settle(rows, t, 0.5 * (clipped(rows, t) + behind))
        return _

    def alone(i, _):
        rows = pl.ds(pl.multiple_of(i * PART, PART), PART)
        t = t_in[rows, :]
        settle(rows, t, clipped(rows, t))
        return _

    lax.fori_loop(0, COUPLE // PART, coupled, 0)
    lax.fori_loop(COUPLE // PART, start_row // PART, alone, 0)
    lax.fori_loop(0, BOUND // PART, starting, 0)
    lax.fori_loop((start_row + BOUND) // PART, size // PART, alone, 0)

    def solve(rows):
        t = jnp.dot(kkt[rows, :], v[...], preferred_element_type=jnp.float32) + t_out[rows, :]
        t_out[rows, :] = t
        return t

    def sent(i, _):
        rows = pl.ds(pl.multiple_of(i * TILE, TILE), TILE)
        y_out[rows, :] = clipped(rows, solve(rows))
        return _

    def kept(i, _):
        solve(pl.ds(pl.multiple_of(i * TILE, TILE), TILE))
        return _

    lax.fori_loop(0, start_row // TILE, sent, 0)
    lax.fori_loop(start_row // TILE, size // TILE, kept, 0)


def run_update(half_link, kkt, costs, bounds, t, got, before):
    size, columns = costs.shape
    inside = pl.BlockSpec(memory_space=pltpu.VMEM)
    return pl.pallas_call(
        update,
        out_shape=(
            jax.ShapeDtypeStruct(t.shape, t.dtype),
            jax.ShapeDtypeStruct((COUPLE + BOUND, columns), t.dtype),
        ),
        in_specs=[pl.BlockSpec(memory_space=pltpu.SMEM)] + [inside] * 6,
        out_specs=(inside,) * 2,
        scratch_shapes=[pltpu.VMEM((size, columns), jnp.bfloat16)],
        input_output_aliases={4: 0},
        compiler_params=pltpu.CompilerParams(vmem_limit_bytes=24 * 1024 * 1024),
        cost_estimate=pl.CostEstimate(
            flops=2 * size * size * columns, bytes_accessed=2 * size * size, transcendentals=0),
        name="update",
    )(half_link, kkt, costs, bounds, t, got, before)


def local(kkt, offsets, lower, upper, partners, adjacency):
    matrix = kkt[0, 0]
    costs = offsets[0, 0]
    low = lower[0, 0]
    high = upper[0, 0]
    bounds = jnp.stack([low, high], axis=1)
    area = lax.axis_index("area")
    win = lax.axis_index("win")
    count = lax.axis_size("area")
    windows = lax.axis_size("win")
    colours = partners[:, 0]
    mates = jnp.bitwise_xor(colours, area)
    linked = jnp.sum(
        jnp.where(mates[:, None] == jnp.arange(count)[None, :], adjacency[area][None, :], 0), axis=1) == 1
    half_links = 0.5 * linked.astype(costs.dtype)
    branches = [functools.partial(run_exchange, colour=c, windows=windows) for c in range(1, count)]

    def step(k, state):
        t, got, before = state
        half_link = lax.dynamic_slice_in_dim(half_links, jnp.maximum(k - 1, 0), 1)
        t, y = run_update(half_link, matrix, costs, bounds, t, got, before)
        got, before = lax.switch(colours[k] - 1, branches, y)
        return t, got, before

    columns = costs.shape[1]
    t, got, before = lax.fori_loop(0, ITERS, step, (
        jnp.zeros_like(costs), jnp.zeros((COUPLE, columns), costs.dtype), jnp.zeros((BOUND, columns), costs.dtype)))
    y = jnp.minimum(jnp.maximum(t, low[:, None]), high[:, None])
    couple = y[:COUPLE]
    first = COUPLE + BOUND
    z = jnp.concatenate([
        couple + half_links[ITERS - 1] * (got - couple),
        y[COUPLE:first],
        0.5 * (y[first:first + BOUND] + jnp.where(win > 0, before, 0.0)),
        y[first + BOUND:],
    ], axis=0)
    return (z[None, None], (t - z)[None, None])


def solution(mesh):
    in_specs = (
        P("area", "win", None, None),
        P("area", "win", None, None),
        P("area", "win", None),
        P("area", "win", None),
        P(),
        P(),
    )
    out_specs = (P("area", "win", None, None), P("area", "win", None, None))
    return jax.shard_map(local, mesh=mesh, in_specs=in_specs, out_specs=out_specs, check_vma=False)
```

```python
import functools

import jax
import jax.numpy as jnp
from jax import lax
from jax.experimental import pallas as pl
from jax.experimental.pallas import tpu as pltpu
from jax.sharding import PartitionSpec as P

COUPLE = 512
BOUND = 256
ITERS = 4
TILE = 512
PART = 128
MESH = pl.DeviceIdType.MESH


def mate_of(area, colour):
    mate = area
    bit = 1
    while bit <= colour:
        if colour & bit:
            mate = mate + bit - 2 * bit * lax.rem(lax.div(area, bit), 2)
        bit *= 2
    return mate


def exchange(colour, windows, y, inbox, send, recv):
    area = lax.axis_index("area")
    win = lax.axis_index("win")
    mate = mate_of(area, colour)
    barrier = pltpu.get_barrier_semaphore()
    pl.semaphore_signal(barrier, inc=1, device_id=(mate, win), device_id_type=MESH)

    @pl.when(win > 0)
    def _():
        pl.semaphore_signal(barrier, inc=1, device_id=(area, win - 1), device_id_type=MESH)

    @pl.when(win < windows - 1)
    def _():
        pl.semaphore_wait(barrier, 2)

    @pl.when(win == windows - 1)
    def _():
        pl.semaphore_wait(barrier, 1)

    couple = pltpu.make_async_remote_copy(
        src_ref=y.at[pl.ds(0, COUPLE)], dst_ref=inbox.at[pl.ds(0, COUPLE)], send_sem=send.at[0], recv_sem=recv.at[0],
        device_id=(mate, win), device_id_type=MESH)
    ends = pltpu.make_async_remote_copy(
        src_ref=y.at[pl.ds(COUPLE, BOUND)], dst_ref=inbox.at[pl.ds(COUPLE, BOUND)], send_sem=send.at[1], recv_sem=recv.at[1],
        device_id=(area, win + 1), device_id_type=MESH)
    couple.start()

    @pl.when(win < windows - 1)
    def _():
        ends.start()

    @pl.when(win > 0)
    def _():
        ends.wait_recv()

    @pl.when(win < windows - 1)
    def _():
        ends.wait_send()

    couple.wait()


def run_exchange(y, *, colour, windows):
    columns = y.shape[1]
    anywhere = pl.BlockSpec(memory_space=pl.ANY)
    return pl.pallas_call(
        functools.partial(exchange, colour, windows),
        out_shape=jax.ShapeDtypeStruct((COUPLE + BOUND, columns), y.dtype),
        in_specs=[anywhere],
        out_specs=anywhere,
        scratch_shapes=[pltpu.SemaphoreType.DMA((2,)), pltpu.SemaphoreType.DMA((2,))],
        compiler_params=pltpu.CompilerParams(
            collective_id=colour, has_side_effects=True, vmem_limit_bytes=1024 * 1024),
        name="exchange_%d" % colour,
    )(y)


def update(step, link, partners, adjacency, kkt, costs, bounds_in, t_in, inbox_in,
           t_out, y_out, next_step, next_link, colour, kk, bounds, inbox, v, load_kkt, load):
    area = lax.axis_index("area")
    win = lax.axis_index("win")
    size = kk.shape[0]
    tiles = size // TILE
    start_row = COUPLE + BOUND

    limits = pltpu.make_async_copy(bounds_in, bounds, load.at[0])
    mail = pltpu.make_async_copy(inbox_in, inbox, load.at[1])
    limits.start()
    mail.start()

    def tile_of_kkt(i):
        rows = pl.ds(pl.multiple_of(i * TILE, TILE), TILE)
        return pltpu.make_async_copy(kkt.at[rows], kk.at[rows], load_kkt.at[i])

    for i in range(tiles):
        tile_of_kkt(i).start()

    now = step[0]
    next_step[0] = now + 1
    colour[0] = partners[now, 0] - 1
    next_link[0] = jnp.where(adjacency[area, partners[now, area]] == 1, 0.5, 0.0)
    has_before = jnp.logical_and(win > 0, now > 0)

    def clipped(rows, t):
        return jnp.minimum(jnp.maximum(t, bounds[rows, 0:1]), bounds[rows, 1:2])

    def settle(rows, t, z):
        u = t - z
        t_out[rows, :] = u
        v[rows, :] = (costs[rows, :] + z - u).astype(v.dtype)

    def coupled(i, _):
        rows = pl.ds(pl.multiple_of(i * PART, PART), PART)
        t = t_in[rows, :]
        y = clipped(rows, t)
        settle(rows, t, y + link[0] * (inbox[rows, :] - y))
        return _

    def starting(i, _):
        rows = pl.ds(pl.multiple_of(start_row + i * PART, PART), PART)
        t = t_in[rows, :]
        before = inbox[pl.ds(pl.multiple_of(COUPLE + i * PART, PART), PART), :]
        settle(rows, t, 0.5 * (clipped(rows, t) + jnp.where(has_before, before, 0.0)))
        return _

    def alone(i, _):
        rows = pl.ds(pl.multiple_of(i * PART, PART), PART)
        t = t_in[rows, :]
        settle(rows, t, clipped(rows, t))
        return _

    limits.wait()
    lax.fori_loop(COUPLE // PART, start_row // PART, alone, 0)
    lax.fori_loop((start_row + BOUND) // PART, size // PART, alone, 0)
    mail.wait()
    lax.fori_loop(0, BOUND // PART, starting, 0)
    lax.fori_loop(0, COUPLE // PART, coupled, 0)

    def solve(i, _):
        rows = pl.ds(pl.multiple_of(i * TILE, TILE), TILE)
        tile_of_kkt(i).wait()
        t = jnp.dot(kk[rows, :], v[...], preferred_element_type=jnp.float32) + t_out[rows, :]
        t_out[rows, :] = t
        y_out[rows, :] = clipped(rows, t)
        return _

    lax.fori_loop(0, tiles, solve, 0)


def run_update(step, link, partners, adjacency, kkt, costs, bounds, t, inbox):
    size, columns = costs.shape
    number = pl.BlockSpec(memory_space=pltpu.SMEM)
    inside = pl.BlockSpec(memory_space=pltpu.VMEM)
    anywhere = pl.BlockSpec(memory_space=pl.ANY)
    return pl.pallas_call(
        update,
        out_shape=(
            jax.ShapeDtypeStruct(t.shape, t.dtype),
            jax.ShapeDtypeStruct(t.shape, t.dtype),
            jax.ShapeDtypeStruct(step.shape, step.dtype),
            jax.ShapeDtypeStruct(link.shape, link.dtype),
            jax.ShapeDtypeStruct(step.shape, step.dtype),
        ),
        in_specs=[number] * 4 + [anywhere, inside, anywhere, inside, anywhere],
        out_specs=(inside, inside, number, number, number),
        scratch_shapes=[
            pltpu.VMEM(kkt.shape, kkt.dtype),
            pltpu.VMEM(bounds.shape, bounds.dtype),
            pltpu.VMEM(inbox.shape, inbox.dtype),
            pltpu.VMEM((size, columns), jnp.bfloat16),
            pltpu.SemaphoreType.DMA((size // TILE,)),
            pltpu.SemaphoreType.DMA((2,)),
        ],
        input_output_aliases={7: 0},
        compiler_params=pltpu.CompilerParams(vmem_limit_bytes=24 * 1024 * 1024),
        cost_estimate=pl.CostEstimate(
            flops=2 * size * size * columns, bytes_accessed=2 * size * size, transcendentals=0),
        name="update",
    )(step, link, partners, adjacency, kkt, costs, bounds, t, inbox)


def local(kkt, offsets, lower, upper, partners, adjacency):
    matrix = kkt[0, 0]
    costs = offsets[0, 0]
    bounds = jnp.stack([lower[0, 0], upper[0, 0]], axis=1)
    win = lax.axis_index("win")
    count = lax.axis_size("area")
    windows = lax.axis_size("win")
    branches = [functools.partial(run_exchange, colour=c, windows=windows) for c in range(1, count)]

    def iterate(_, state):
        t, y, inbox, step, link = state
        t, y, step, link, colour = run_update(step, link, partners, adjacency, matrix, costs, bounds, t, inbox)
        inbox = lax.switch(colour[0], branches, y)
        return t, y, inbox, step, link

    columns = costs.shape[1]
    zeros = jnp.zeros_like(costs)
    t, y, inbox, _, link = lax.fori_loop(0, ITERS, iterate, (
        zeros, zeros, jnp.zeros((COUPLE + BOUND, columns), costs.dtype),
        jnp.zeros((1,), jnp.int32), jnp.zeros((1,), costs.dtype)))
    couple = y[:COUPLE]
    first = COUPLE + BOUND
    z = jnp.concatenate([
        couple + link[0] * (inbox[:COUPLE] - couple),
        y[COUPLE:first],
        0.5 * (y[first:first + BOUND] + jnp.where(win > 0, inbox[COUPLE:], 0.0)),
        y[first + BOUND:],
    ], axis=0)
    return (z[None, None], (t - z)[None, None])


def solution(mesh):
    in_specs = (
        P("area", "win", None, None),
        P("area", "win", None, None),
        P("area", "win", None),
        P("area", "win", None),
        P(),
        P(),
    )
    out_specs = (P("area", "win", None, None), P("area", "win", None, None))
    return jax.shard_map(local, mesh=mesh, in_specs=in_specs, out_specs=out_specs, check_vma=False)
```

```python
import functools

import jax
import jax.numpy as jnp
from jax import lax
from jax.experimental import pallas as pl
from jax.experimental.pallas import tpu as pltpu
from jax.sharding import PartitionSpec as P

COUPLE = 512
BOUND = 256
ITERS = 4
TILE = 512
PART = 128
LANES = 128
MESH = pl.DeviceIdType.MESH


def mate_of(area, colour):
    mate = area
    bit = 1
    while bit <= colour:
        if colour & bit:
            mate = mate + bit - 2 * bit * lax.rem(lax.div(area, bit), 2)
        bit *= 2
    return mate


def exchange(colour, windows, y, inbox, send, recv):
    area = lax.axis_index("area")
    win = lax.axis_index("win")
    mate = mate_of(area, colour)
    barrier = pltpu.get_barrier_semaphore()
    pl.semaphore_signal(barrier, inc=1, device_id=(mate, win), device_id_type=MESH)

    @pl.when(win > 0)
    def _():
        pl.semaphore_signal(barrier, inc=1, device_id=(area, win - 1), device_id_type=MESH)

    @pl.when(win < windows - 1)
    def _():
        pl.semaphore_wait(barrier, 2)

    @pl.when(win == windows - 1)
    def _():
        pl.semaphore_wait(barrier, 1)

    couple = pltpu.make_async_remote_copy(
        src_ref=y.at[pl.ds(0, COUPLE)], dst_ref=inbox.at[pl.ds(0, COUPLE)], send_sem=send.at[0], recv_sem=recv.at[0],
        device_id=(mate, win), device_id_type=MESH)
    ends = pltpu.make_async_remote_copy(
        src_ref=y.at[pl.ds(COUPLE, BOUND)], dst_ref=inbox.at[pl.ds(COUPLE, BOUND)], send_sem=send.at[1], recv_sem=recv.at[1],
        device_id=(area, win + 1), device_id_type=MESH)
    couple.start()

    @pl.when(win < windows - 1)
    def _():
        ends.start()

    @pl.when(win > 0)
    def _():
        ends.wait_recv()

    @pl.when(win < windows - 1)
    def _():
        ends.wait_send()

    couple.wait()


def run_exchange(y, *, colour, windows):
    columns = y.shape[1]
    anywhere = pl.BlockSpec(memory_space=pl.ANY)
    return pl.pallas_call(
        functools.partial(exchange, colour, windows),
        out_shape=jax.ShapeDtypeStruct((COUPLE + BOUND, columns), y.dtype),
        in_specs=[anywhere],
        out_specs=anywhere,
        scratch_shapes=[pltpu.SemaphoreType.DMA((2,)), pltpu.SemaphoreType.DMA((2,))],
        compiler_params=pltpu.CompilerParams(
            collective_id=colour, has_side_effects=True, vmem_limit_bytes=1024 * 1024),
        name="exchange_%d" % colour,
    )(y)


def settle_all(link, low, high, t_in, inbox, mail, has_before, settle):
    start_row = COUPLE + BOUND
    size = t_in.shape[0]

    def clipped_part(i):
        rows = pl.ds(pl.multiple_of(i * PART, PART), PART)
        t = t_in[rows, :]
        return rows, t, clipped(low, high, rows, t)

    def alone(i, _):
        rows, t, y = clipped_part(i)
        settle(rows, i, t, y)
        return _

    def starting(i, _):
        rows, t, y = clipped_part(start_row // PART + i)
        before = inbox[pl.ds(pl.multiple_of(COUPLE + i * PART, PART), PART), :]
        settle(rows, start_row // PART + i, t, 0.5 * (y + jnp.where(has_before, before, 0.0)))
        return _

    def coupled(i, _):
        rows, t, y = clipped_part(i)
        settle(rows, i, t, y + link[0] * (inbox[rows, :] - y))
        return _

    lax.fori_loop(COUPLE // PART, start_row // PART, alone, 0)
    lax.fori_loop((start_row + BOUND) // PART, size // PART, alone, 0)
    mail.wait()
    lax.fori_loop(0, BOUND // PART, starting, 0)
    lax.fori_loop(0, COUPLE // PART, coupled, 0)


def clipped(low, high, rows, t):
    repeats = t.shape[1] // LANES
    least = jnp.concatenate([low[rows, :]] * repeats, axis=1)
    most = jnp.concatenate([high[rows, :]] * repeats, axis=1)
    return jnp.minimum(jnp.maximum(t, least), most)


def update(step, link, partners, adjacency, kkt, costs, low, high, t_in, inbox_in,
           t_out, y_out, next_step, next_link, colour, inbox, v, load):
    area = lax.axis_index("area")
    win = lax.axis_index("win")
    mail = pltpu.make_async_copy(inbox_in, inbox, load)
    mail.start()
    now = step[0]
    next_step[0] = now + 1
    colour[0] = partners[now, 0] - 1
    next_link[0] = jnp.where(adjacency[area, partners[now, area]] == 1, 0.5, 0.0)

    def settle(rows, part, t, z):
        u = t - z
        t_out[rows, :] = u
        v[rows, :] = (costs[rows, :] + z - u).astype(v.dtype)

    settle_all(link, low, high, t_in, inbox, mail, jnp.logical_and(win > 0, now > 0), settle)

    def solve(i, _):
        rows = pl.ds(pl.multiple_of(i * TILE, TILE), TILE)
        t = jnp.dot(kkt[rows, :], v[...], preferred_element_type=jnp.float32) + t_out[rows, :]
        t_out[rows, :] = t
        y_out[rows, :] = clipped(low, high, rows, t)
        return _

    lax.fori_loop(0, kkt.shape[0] // TILE, solve, 0)


def finish(link, low, high, t_in, inbox_in, z_out, u_out, inbox, z_kept, u_kept, load, done):
    mail = pltpu.make_async_copy(inbox_in, inbox, load)
    mail.start()

    def leaving(part):
        rows = pl.ds(pl.multiple_of(part * PART, PART), PART)
        return (pltpu.make_async_copy(z_kept.at[rows], z_out.at[rows], done.at[0, part]),
                pltpu.make_async_copy(u_kept.at[rows], u_out.at[rows], done.at[1, part]))

    def settle(rows, part, t, z):
        z_kept[rows, :] = z
        u_kept[rows, :] = t - z
        for copy in leaving(part):
            copy.start()

    settle_all(link, low, high, t_in, inbox, mail, lax.axis_index("win") > 0, settle)

    def gone(part, _):
        for copy in leaving(part):
            copy.wait()
        return _

    lax.fori_loop(0, t_in.shape[0] // PART, gone, 0)


def run_finish(link, low, high, t, inbox):
    inside = pl.BlockSpec(memory_space=pltpu.VMEM)
    anywhere = pl.BlockSpec(memory_space=pl.ANY)
    like = jax.ShapeDtypeStruct(t.shape, t.dtype)
    return pl.pallas_call(
        finish,
        out_shape=(like, like),
        in_specs=[pl.BlockSpec(memory_space=pltpu.SMEM), inside, inside, inside, anywhere],
        out_specs=(anywhere, anywhere),
        scratch_shapes=[
            pltpu.VMEM(inbox.shape, inbox.dtype),
            pltpu.VMEM(t.shape, t.dtype),
            pltpu.VMEM(t.shape, t.dtype),
            pltpu.SemaphoreType.DMA,
            pltpu.SemaphoreType.DMA((2, t.shape[0] // PART)),
        ],
        compiler_params=pltpu.CompilerParams(vmem_limit_bytes=16 * 1024 * 1024),
        name="finish",
    )(link, low, high, t, inbox)


def run_update(step, link, partners, adjacency, kkt, costs, low, high, t, inbox):
    size, columns = costs.shape
    number = pl.BlockSpec(memory_space=pltpu.SMEM)
    inside = pl.BlockSpec(memory_space=pltpu.VMEM)
    kkt, low, high = (pltpu.with_memory_space_constraint(a, pltpu.VMEM) for a in (kkt, low, high))
    return pl.pallas_call(
        update,
        out_shape=(
            jax.ShapeDtypeStruct(t.shape, t.dtype),
            jax.ShapeDtypeStruct(t.shape, t.dtype),
            jax.ShapeDtypeStruct(step.shape, step.dtype),
            jax.ShapeDtypeStruct(link.shape, link.dtype),
            jax.ShapeDtypeStruct(step.shape, step.dtype),
        ),
        in_specs=[number] * 4 + [inside] * 5 + [pl.BlockSpec(memory_space=pl.ANY)],
        out_specs=(inside, inside, number, number, number),
        scratch_shapes=[
            pltpu.VMEM(inbox.shape, inbox.dtype),
            pltpu.VMEM((size, columns), jnp.bfloat16),
            pltpu.SemaphoreType.DMA,
        ],
        input_output_aliases={8: 0},
        compiler_params=pltpu.CompilerParams(vmem_limit_bytes=16 * 1024 * 1024),
        cost_estimate=pl.CostEstimate(
            flops=2 * size * size * columns, bytes_accessed=2 * size * size, transcendentals=0),
        name="update",
    )(step, link, partners, adjacency, kkt, costs, low, high, t, inbox)


def keep(kkt, bounds, kk, low, high, done):
    size = kkt.shape[0]

    def tile_of_kkt(i):
        rows = pl.ds(i * PART, PART)
        return pltpu.make_async_copy(kkt.at[rows], kk.at[rows], done.at[i])

    for i in range(size // PART):
        tile_of_kkt(i).start()

    def spread(i, _):
        rows = pl.ds(pl.multiple_of(i * PART, PART), PART)
        low[rows, :] = jnp.broadcast_to(bounds[rows, 0:1], (PART, low.shape[1]))
        high[rows, :] = jnp.broadcast_to(bounds[rows, 1:2], (PART, low.shape[1]))
        return _

    lax.fori_loop(0, size // PART, spread, 0)
    for i in range(size // PART):
        tile_of_kkt(i).wait()


def run_keep(kkt, bounds):
    size = kkt.shape[0]
    inside = pl.BlockSpec(memory_space=pltpu.VMEM)
    return pl.pallas_call(
        keep,
        out_shape=(
            pltpu.VMEM(kkt.shape, kkt.dtype),
            pltpu.VMEM((size, LANES), bounds.dtype),
            pltpu.VMEM((size, LANES), bounds.dtype),
        ),
        in_specs=[pl.BlockSpec(memory_space=pl.ANY), inside],
        out_specs=(inside,) * 3,
        scratch_shapes=[pltpu.SemaphoreType.DMA((size // PART,))],
        compiler_params=pltpu.CompilerParams(vmem_limit_bytes=4 * 1024 * 1024),
        name="keep",
    )(pltpu.with_memory_space_constraint(kkt, pltpu.HBM), bounds)


def local(kkt, offsets, lower, upper, partners, adjacency):
    costs = offsets[0, 0]
    matrix, low, high = run_keep(kkt[0, 0], jnp.stack([lower[0, 0], upper[0, 0]], axis=1))
    count = lax.axis_size("area")
    windows = lax.axis_size("win")
    branches = [functools.partial(run_exchange, colour=c, windows=windows) for c in range(1, count)]

    def iterate(_, state):
        t, inbox, step, link = state
        t, y, step, link, colour = run_update(step, link, partners, adjacency, matrix, costs, low, high, t, inbox)
        inbox = lax.switch(colour[0], branches, y)
        return t, inbox, step, link

    t, inbox, _, link = lax.fori_loop(0, ITERS, iterate, (
        jnp.zeros_like(costs), jnp.zeros((COUPLE + BOUND, costs.shape[1]), costs.dtype),
        jnp.zeros((1,), jnp.int32), jnp.zeros((1,), costs.dtype)))
    z, u = run_finish(link, low, high, t, inbox)
    return (z[None, None], u[None, None])


def solution(mesh):
    in_specs = (
        P("area", "win", None, None),
        P("area", "win", None, None),
        P("area", "win", None),
        P("area", "win", None),
        P(),
        P(),
    )
    out_specs = (P("area", "win", None, None), P("area", "win", None, None))
    return jax.shard_map(local, mesh=mesh, in_specs=in_specs, out_specs=out_specs, check_vma=False)
```

```python
import functools

import jax
import jax.numpy as jnp
from jax import lax
from jax.experimental import pallas as pl
from jax.experimental.pallas import tpu as pltpu
from jax.sharding import PartitionSpec as P

COUPLE = 512
BOUND = 256
ITERS = 4
TILE = 256
PART = 128
MESH = pl.DeviceIdType.MESH


def mate_of(area, colour):
    mate = area
    bit = 1
    while bit <= colour:
        if colour & bit:
            mate = mate + bit - 2 * bit * lax.rem(lax.div(area, bit), 2)
        bit *= 2
    return mate


def exchange(colour, windows, y, inbox, send, recv):
    area = lax.axis_index("area")
    win = lax.axis_index("win")
    mate = mate_of(area, colour)
    barrier = pltpu.get_barrier_semaphore()
    pl.semaphore_signal(barrier, inc=1, device_id=(mate, win), device_id_type=MESH)

    @pl.when(win > 0)
    def _():
        pl.semaphore_signal(barrier, inc=1, device_id=(area, win - 1), device_id_type=MESH)

    @pl.when(win < windows - 1)
    def _():
        pl.semaphore_wait(barrier, 2)

    @pl.when(win == windows - 1)
    def _():
        pl.semaphore_wait(barrier, 1)

    couple = pltpu.make_async_remote_copy(
        src_ref=y.at[pl.ds(0, COUPLE)], dst_ref=inbox.at[pl.ds(0, COUPLE)], send_sem=send.at[0], recv_sem=recv.at[0],
        device_id=(mate, win), device_id_type=MESH)
    ends = pltpu.make_async_remote_copy(
        src_ref=y.at[pl.ds(COUPLE, BOUND)], dst_ref=inbox.at[pl.ds(COUPLE, BOUND)], send_sem=send.at[1], recv_sem=recv.at[1],
        device_id=(area, win + 1), device_id_type=MESH)
    couple.start()

    @pl.when(win < windows - 1)
    def _():
        ends.start()

    @pl.when(win > 0)
    def _():
        ends.wait_recv()

    @pl.when(win < windows - 1)
    def _():
        ends.wait_send()

    couple.wait()


def run_exchange(y, *, colour, windows):
    columns = y.shape[1]
    anywhere = pl.BlockSpec(memory_space=pl.ANY)
    return pl.pallas_call(
        functools.partial(exchange, colour, windows),
        out_shape=jax.ShapeDtypeStruct((COUPLE + BOUND, columns), y.dtype),
        in_specs=[anywhere],
        out_specs=anywhere,
        scratch_shapes=[pltpu.SemaphoreType.DMA((2,)), pltpu.SemaphoreType.DMA((2,))],
        compiler_params=pltpu.CompilerParams(
            collective_id=colour, has_side_effects=True, vmem_limit_bytes=1024 * 1024),
        name="exchange_%d" % colour,
    )(y)


def settle_all(scalars, bounds, t_in, inbox, limits, mail, has_before, settle):
    start_row = COUPLE + BOUND
    size = t_in.shape[0]
    half_link = 0.5 * scalars[1].astype(jnp.float32)

    def clipped_part(i):
        rows = pl.ds(pl.multiple_of(i * PART, PART), PART)
        t = t_in[rows, :]
        return rows, t, clipped(bounds, rows, t)

    def alone(i, _):
        rows, t, y = clipped_part(i)
        settle(rows, i, t, y)
        return _

    def starting(i, _):
        rows, t, y = clipped_part(start_row // PART + i)
        before = inbox[pl.ds(pl.multiple_of(COUPLE + i * PART, PART), PART), :]
        settle(rows, start_row // PART + i, t, 0.5 * (y + jnp.where(has_before, before, 0.0)))
        return _

    def coupled(i, _):
        rows, t, y = clipped_part(i)
        settle(rows, i, t, y + half_link * (inbox[rows, :] - y))
        return _

    limits.wait()
    lax.fori_loop(COUPLE // PART, start_row // PART, alone, 0)
    lax.fori_loop((start_row + BOUND) // PART, size // PART, alone, 0)
    mail.wait()
    lax.fori_loop(0, BOUND // PART, starting, 0)
    lax.fori_loop(0, COUPLE // PART, coupled, 0)


def clipped(bounds, rows, t):
    return jnp.minimum(jnp.maximum(t, bounds[rows, 0:1]), bounds[rows, 1:2])


def update(scalars, partners, adjacency, kkt, costs, bounds_in, t_in, inbox_in,
           t_out, y_out, next_scalars, colour, kk, bounds, inbox, v, load_kkt, load):
    area = lax.axis_index("area")
    win = lax.axis_index("win")
    tiles = kk.shape[0] // TILE
    limits = pltpu.make_async_copy(bounds_in, bounds, load.at[0])
    mail = pltpu.make_async_copy(inbox_in, inbox, load.at[1])
    limits.start()
    mail.start()

    def tile_of_kkt(i):
        rows = pl.ds(pl.multiple_of(i * TILE, TILE), TILE)
        return pltpu.make_async_copy(kkt.at[rows], kk.at[rows], load_kkt.at[i])

    for i in range(tiles):
        tile_of_kkt(i).start()

    now = scalars[0]
    next_scalars[0] = now + 1
    next_scalars[1] = jnp.where(adjacency[area, partners[now, area]] == 1, 1, 0)
    colour[0] = partners[now, 0] - 1

    def settle(rows, part, t, z):
        u = t - z
        t_out[rows, :] = u
        v[rows, :] = (costs[rows, :] + z - u).astype(v.dtype)

    settle_all(scalars, bounds, t_in, inbox, limits, mail, jnp.logical_and(win > 0, now > 0), settle)

    def solve(i, _):
        rows = pl.ds(pl.multiple_of(i * TILE, TILE), TILE)
        tile_of_kkt(i).wait()
        t = jnp.dot(kk[rows, :], v[...], preferred_element_type=jnp.float32) + t_out[rows, :]
        t_out[rows, :] = t

        @pl.when(i < y_out.shape[0] // TILE)
        def _():
            y_out[rows, :] = clipped(bounds, rows, t)

        return 0

    lax.fori_loop(0, tiles, solve, 0)


def finish(scalars, bounds_in, t_in, inbox_in, z_out, u_out, bounds, inbox, z_kept, u_kept, load, done):
    limits = pltpu.make_async_copy(bounds_in, bounds, load.at[0])
    mail = pltpu.make_async_copy(inbox_in, inbox, load.at[1])
    limits.start()
    mail.start()

    def leaving(part):
        rows = pl.ds(pl.multiple_of(part * PART, PART), PART)
        return (pltpu.make_async_copy(z_kept.at[rows], z_out.at[rows], done.at[0, part]),
                pltpu.make_async_copy(u_kept.at[rows], u_out.at[rows], done.at[1, part]))

    def settle(rows, part, t, z):
        z_kept[rows, :] = z
        u_kept[rows, :] = t - z
        for copy in leaving(part):
            copy.start()

    settle_all(scalars, bounds, t_in, inbox, limits, mail, lax.axis_index("win") > 0, settle)

    def gone(part, _):
        for copy in leaving(part):
            copy.wait()
        return _

    lax.fori_loop(0, t_in.shape[0] // PART, gone, 0)


def run_finish(scalars, bounds, t, inbox):
    inside = pl.BlockSpec(memory_space=pltpu.VMEM)
    anywhere = pl.BlockSpec(memory_space=pl.ANY)
    like = jax.ShapeDtypeStruct(t.shape, t.dtype)
    return pl.pallas_call(
        finish,
        out_shape=(like, like),
        in_specs=[pl.BlockSpec(memory_space=pltpu.SMEM), anywhere, inside, anywhere],
        out_specs=(anywhere, anywhere),
        scratch_shapes=[
            pltpu.VMEM(bounds.shape, bounds.dtype),
            pltpu.VMEM(inbox.shape, inbox.dtype),
            pltpu.VMEM(t.shape, t.dtype),
            pltpu.VMEM(t.shape, t.dtype),
            pltpu.SemaphoreType.DMA((2,)),
            pltpu.SemaphoreType.DMA((2, t.shape[0] // PART)),
        ],
        compiler_params=pltpu.CompilerParams(vmem_limit_bytes=16 * 1024 * 1024),
        name="finish",
    )(scalars, bounds, t, inbox)


def run_update(scalars, partners, adjacency, kkt, costs, bounds, t, inbox):
    size, columns = costs.shape
    number = pl.BlockSpec(memory_space=pltpu.SMEM)
    inside = pl.BlockSpec(memory_space=pltpu.VMEM)
    anywhere = pl.BlockSpec(memory_space=pl.ANY)
    return pl.pallas_call(
        update,
        out_shape=(
            jax.ShapeDtypeStruct(t.shape, t.dtype),
            jax.ShapeDtypeStruct((COUPLE + BOUND, columns), t.dtype),
            jax.ShapeDtypeStruct(scalars.shape, scalars.dtype),
            jax.ShapeDtypeStruct((1,), jnp.int32),
        ),
        in_specs=[number] * 3 + [anywhere, inside, anywhere, inside, anywhere],
        out_specs=(inside, inside, number, number),
        scratch_shapes=[
            pltpu.VMEM(kkt.shape, kkt.dtype),
            pltpu.VMEM(bounds.shape, bounds.dtype),
            pltpu.VMEM(inbox.shape, inbox.dtype),
            pltpu.VMEM((size, columns), jnp.bfloat16),
            pltpu.SemaphoreType.DMA((size // TILE,)),
            pltpu.SemaphoreType.DMA((2,)),
        ],
        input_output_aliases={6: 0},
        compiler_params=pltpu.CompilerParams(vmem_limit_bytes=24 * 1024 * 1024),
        cost_estimate=pl.CostEstimate(
            flops=2 * size * size * columns, bytes_accessed=2 * size * size, transcendentals=0),
        name="update",
    )(scalars, partners, adjacency, kkt, costs, bounds, t, inbox)


def local(kkt, offsets, lower, upper, partners, adjacency):
    costs = offsets[0, 0]
    matrix = kkt[0, 0]
    bounds = jnp.stack([lower[0, 0], upper[0, 0]], axis=1)
    count = lax.axis_size("area")
    windows = lax.axis_size("win")
    branches = [functools.partial(run_exchange, colour=c, windows=windows) for c in range(1, count)]

    def iterate(_, state):
        t, inbox, scalars = state
        t, y, scalars, colour = run_update(scalars, partners, adjacency, matrix, costs, bounds, t, inbox)
        inbox = lax.switch(colour[0], branches, y)
        return t, inbox, scalars

    t, inbox, scalars = lax.fori_loop(0, ITERS, iterate, (
        jnp.zeros_like(costs), jnp.zeros((COUPLE + BOUND, costs.shape[1]), costs.dtype), jnp.zeros((2,), jnp.int32)))
    z, u = run_finish(scalars, bounds, t, inbox)
    return (z[None, None], u[None, None])


def solution(mesh):
    in_specs = (
        P("area", "win", None, None),
        P("area", "win", None, None),
        P("area", "win", None),
        P("area", "win", None),
        P(),
        P(),
    )
    out_specs = (P("area", "win", None, None), P("area", "win", None, None))
    return jax.shard_map(local, mesh=mesh, in_specs=in_specs, out_specs=out_specs, check_vma=False)
```

```python
import functools

import jax
import jax.numpy as jnp
from jax import lax
from jax.experimental import pallas as pl
from jax.experimental.pallas import tpu as pltpu
from jax.sharding import PartitionSpec as P

COUPLE = 512
BOUND = 256
ITERS = 4
TILE = 768
PART = 128
MESH = pl.DeviceIdType.MESH


def mate_of(area, colour):
    mate = area
    bit = 1
    while bit <= colour:
        if colour & bit:
            mate = mate + bit - 2 * bit * lax.rem(lax.div(area, bit), 2)
        bit *= 2
    return mate


def exchange(colour, windows, y, inbox, send, recv):
    area = lax.axis_index("area")
    win = lax.axis_index("win")
    mate = mate_of(area, colour)
    barrier = pltpu.get_barrier_semaphore()
    pl.semaphore_signal(barrier, inc=1, device_id=(mate, win), device_id_type=MESH)

    @pl.when(win > 0)
    def _():
        pl.semaphore_signal(barrier, inc=1, device_id=(area, win - 1), device_id_type=MESH)

    @pl.when(win < windows - 1)
    def _():
        pl.semaphore_wait(barrier, 2)

    @pl.when(win == windows - 1)
    def _():
        pl.semaphore_wait(barrier, 1)

    couple = pltpu.make_async_remote_copy(
        src_ref=y.at[pl.ds(0, COUPLE)], dst_ref=inbox.at[pl.ds(0, COUPLE)], send_sem=send.at[0], recv_sem=recv.at[0],
        device_id=(mate, win), device_id_type=MESH)
    ends = pltpu.make_async_remote_copy(
        src_ref=y.at[pl.ds(COUPLE, BOUND)], dst_ref=inbox.at[pl.ds(COUPLE, BOUND)], send_sem=send.at[1], recv_sem=recv.at[1],
        device_id=(area, win + 1), device_id_type=MESH)
    couple.start()

    @pl.when(win < windows - 1)
    def _():
        ends.start()

    @pl.when(win > 0)
    def _():
        ends.wait_recv()

    @pl.when(win < windows - 1)
    def _():
        ends.wait_send()

    couple.wait()


def run_exchange(y, *, colour, windows):
    columns = y.shape[1]
    anywhere = pl.BlockSpec(memory_space=pl.ANY)
    return pl.pallas_call(
        functools.partial(exchange, colour, windows),
        out_shape=jax.ShapeDtypeStruct((COUPLE + BOUND, columns), y.dtype),
        in_specs=[anywhere],
        out_specs=anywhere,
        scratch_shapes=[pltpu.SemaphoreType.DMA((2,)), pltpu.SemaphoreType.DMA((2,))],
        compiler_params=pltpu.CompilerParams(
            collective_id=colour, has_side_effects=True, vmem_limit_bytes=1024 * 1024),
        name="exchange_%d" % colour,
    )(y)


def settle_all(scalars, bounds, t_in, inbox, limits, mail, has_before, settle):
    start_row = COUPLE + BOUND
    size = t_in.shape[0]
    half_link = 0.5 * scalars[1].astype(jnp.float32)

    def clipped_part(i):
        rows = pl.ds(pl.multiple_of(i * PART, PART), PART)
        t = t_in[rows, :]
        return rows, t, clipped(bounds, rows, t)

    def alone(i, _):
        rows, t, y = clipped_part(i)
        settle(rows, i, t, y)
        return _

    def starting(i, _):
        rows, t, y = clipped_part(start_row // PART + i)
        before = inbox[pl.ds(pl.multiple_of(COUPLE + i * PART, PART), PART), :]
        settle(rows, start_row // PART + i, t, 0.5 * (y + jnp.where(has_before, before, 0.0)))
        return _

    def coupled(i, _):
        rows, t, y = clipped_part(i)
        settle(rows, i, t, y + half_link * (inbox[rows, :] - y))
        return _

    limits.wait()
    lax.fori_loop(COUPLE // PART, start_row // PART, alone, 0)
    lax.fori_loop((start_row + BOUND) // PART, size // PART, alone, 0)
    mail.wait()
    lax.fori_loop(0, BOUND // PART, starting, 0)
    lax.fori_loop(0, COUPLE // PART, coupled, 0)


def clipped(bounds, rows, t):
    return jnp.minimum(jnp.maximum(t, bounds[rows, 0:1]), bounds[rows, 1:2])


def update(scalars, partners, adjacency, kkt, costs, bounds_in, t_in, inbox_in,
           t_out, y_out, next_scalars, colour, kk, bounds, inbox, v, load_kkt, load):
    area = lax.axis_index("area")
    win = lax.axis_index("win")
    tiles = kk.shape[0] // TILE
    limits = pltpu.make_async_copy(bounds_in, bounds, load.at[0])
    mail = pltpu.make_async_copy(inbox_in, inbox, load.at[1])
    limits.start()
    mail.start()

    def part_of_kkt(i):
        rows = pl.ds(pl.multiple_of(i * PART, PART), PART)
        return pltpu.make_async_copy(kkt.at[rows], kk.at[rows], load_kkt.at[i])

    for i in range(tiles * TILE // PART):
        part_of_kkt(i).start()

    now = scalars[0]
    next_scalars[0] = now + 1
    next_scalars[1] = jnp.where(adjacency[area, partners[now, area]] == 1, 1, 0)
    colour[0] = partners[now, 0] - 1

    def settle(rows, part, t, z):
        u = t - z
        t_out[rows, :] = u
        v[rows, :] = (costs[rows, :] + z - u).astype(v.dtype)

    settle_all(scalars, bounds, t_in, inbox, limits, mail, jnp.logical_and(win > 0, now > 0), settle)

    def solve(i, _):
        rows = pl.ds(pl.multiple_of(i * TILE, TILE), TILE)
        for j in range(TILE // PART):
            part_of_kkt(i * (TILE // PART) + j).wait()

        t = jnp.dot(kk[rows, :], v[...], preferred_element_type=jnp.float32) + t_out[rows, :]
        t_out[rows, :] = t

        @pl.when(i < y_out.shape[0] // TILE)
        def _():
            y_out[rows, :] = clipped(bounds, rows, t)

        return 0

    lax.fori_loop(0, tiles, solve, 0)


def finish(scalars, bounds_in, t_in, inbox_in, z_out, u_out, bounds, inbox, z_kept, u_kept, load, done):
    limits = pltpu.make_async_copy(bounds_in, bounds, load.at[0])
    mail = pltpu.make_async_copy(inbox_in, inbox, load.at[1])
    limits.start()
    mail.start()

    def leaving(part):
        rows = pl.ds(pl.multiple_of(part * PART, PART), PART)
        return (pltpu.make_async_copy(z_kept.at[rows], z_out.at[rows], done.at[0, part]),
                pltpu.make_async_copy(u_kept.at[rows], u_out.at[rows], done.at[1, part]))

    def settle(rows, part, t, z):
        z_kept[rows, :] = z
        u_kept[rows, :] = t - z
        for copy in leaving(part):
            copy.start()

    settle_all(scalars, bounds, t_in, inbox, limits, mail, lax.axis_index("win") > 0, settle)

    def gone(part, _):
        for copy in leaving(part):
            copy.wait()
        return _

    lax.fori_loop(0, t_in.shape[0] // PART, gone, 0)


def run_finish(scalars, bounds, t, inbox):
    inside = pl.BlockSpec(memory_space=pltpu.VMEM)
    anywhere = pl.BlockSpec(memory_space=pl.ANY)
    like = jax.ShapeDtypeStruct(t.shape, t.dtype)
    return pl.pallas_call(
        finish,
        out_shape=(like, like),
        in_specs=[pl.BlockSpec(memory_space=pltpu.SMEM), anywhere, inside, anywhere],
        out_specs=(anywhere, anywhere),
        scratch_shapes=[
            pltpu.VMEM(bounds.shape, bounds.dtype),
            pltpu.VMEM(inbox.shape, inbox.dtype),
            pltpu.VMEM(t.shape, t.dtype),
            pltpu.VMEM(t.shape, t.dtype),
            pltpu.SemaphoreType.DMA((2,)),
            pltpu.SemaphoreType.DMA((2, t.shape[0] // PART)),
        ],
        compiler_params=pltpu.CompilerParams(vmem_limit_bytes=16 * 1024 * 1024),
        name="finish",
    )(scalars, bounds, t, inbox)


def run_update(scalars, partners, adjacency, kkt, costs, bounds, t, inbox):
    size, columns = costs.shape
    number = pl.BlockSpec(memory_space=pltpu.SMEM)
    inside = pl.BlockSpec(memory_space=pltpu.VMEM)
    anywhere = pl.BlockSpec(memory_space=pl.ANY)
    return pl.pallas_call(
        update,
        out_shape=(
            jax.ShapeDtypeStruct(t.shape, t.dtype),
            jax.ShapeDtypeStruct((COUPLE + BOUND, columns), t.dtype),
            jax.ShapeDtypeStruct(scalars.shape, scalars.dtype),
            jax.ShapeDtypeStruct((1,), jnp.int32),
        ),
        in_specs=[number] * 3 + [anywhere, inside, anywhere, inside, anywhere],
        out_specs=(inside, inside, number, number),
        scratch_shapes=[
            pltpu.VMEM(kkt.shape, kkt.dtype),
            pltpu.VMEM(bounds.shape, bounds.dtype),
            pltpu.VMEM(inbox.shape, inbox.dtype),
            pltpu.VMEM((size, columns), jnp.bfloat16),
            pltpu.SemaphoreType.DMA((size // PART,)),
            pltpu.SemaphoreType.DMA((2,)),
        ],
        input_output_aliases={6: 0},
        compiler_params=pltpu.CompilerParams(vmem_limit_bytes=24 * 1024 * 1024),
        cost_estimate=pl.CostEstimate(
            flops=2 * size * size * columns, bytes_accessed=2 * size * size, transcendentals=0),
        name="update",
    )(scalars, partners, adjacency, kkt, costs, bounds, t, inbox)


def local(kkt, offsets, lower, upper, partners, adjacency):
    costs = offsets[0, 0]
    matrix = kkt[0, 0]
    bounds = jnp.stack([lower[0, 0], upper[0, 0]], axis=1)
    count = lax.axis_size("area")
    windows = lax.axis_size("win")
    branches = [functools.partial(run_exchange, colour=c, windows=windows) for c in range(1, count)]

    def iterate(_, state):
        t, inbox, scalars = state
        t, y, scalars, colour = run_update(scalars, partners, adjacency, matrix, costs, bounds, t, inbox)
        inbox = lax.switch(colour[0], branches, y)
        return t, inbox, scalars

    t, inbox, scalars = lax.fori_loop(0, ITERS, iterate, (
        jnp.zeros_like(costs), jnp.zeros((COUPLE + BOUND, costs.shape[1]), costs.dtype), jnp.zeros((2,), jnp.int32)))
    z, u = run_finish(scalars, bounds, t, inbox)
    return (z[None, None], u[None, None])


def solution(mesh):
    in_specs = (
        P("area", "win", None, None),
        P("area", "win", None, None),
        P("area", "win", None),
        P("area", "win", None),
        P(),
        P(),
    )
    out_specs = (P("area", "win", None, None), P("area", "win", None, None))
    return jax.shard_map(local, mesh=mesh, in_specs=in_specs, out_specs=out_specs, check_vma=False)
```

```python
import functools

import jax
import jax.numpy as jnp
from jax import lax
from jax.experimental import pallas as pl
from jax.experimental.pallas import tpu as pltpu
from jax.sharding import PartitionSpec as P

COUPLE = 512
BOUND = 256
ITERS = 4
TILE = 768
PART = 128
MESH = pl.DeviceIdType.MESH


def mate_of(area, colour):
    mate = area
    bit = 1
    while bit <= colour:
        if colour & bit:
            mate = mate + bit - 2 * bit * lax.rem(lax.div(area, bit), 2)
        bit *= 2
    return mate


def exchange(colour, windows, y, inbox, send, recv):
    area = lax.axis_index("area")
    win = lax.axis_index("win")
    mate = mate_of(area, colour)
    barrier = pltpu.get_barrier_semaphore()
    pl.semaphore_signal(barrier, inc=1, device_id=(mate, win), device_id_type=MESH)

    @pl.when(win > 0)
    def _():
        pl.semaphore_signal(barrier, inc=1, device_id=(area, win - 1), device_id_type=MESH)

    @pl.when(win < windows - 1)
    def _():
        pl.semaphore_wait(barrier, 2)

    @pl.when(win == windows - 1)
    def _():
        pl.semaphore_wait(barrier, 1)

    couple = pltpu.make_async_remote_copy(
        src_ref=y.at[pl.ds(0, COUPLE)], dst_ref=inbox.at[pl.ds(0, COUPLE)], send_sem=send.at[0], recv_sem=recv.at[0],
        device_id=(mate, win), device_id_type=MESH)
    ends = pltpu.make_async_remote_copy(
        src_ref=y.at[pl.ds(COUPLE, BOUND)], dst_ref=inbox.at[pl.ds(COUPLE, BOUND)], send_sem=send.at[1], recv_sem=recv.at[1],
        device_id=(area, win + 1), device_id_type=MESH)
    couple.start()

    @pl.when(win < windows - 1)
    def _():
        ends.start()

    @pl.when(win > 0)
    def _():
        ends.wait_recv()

    @pl.when(win < windows - 1)
    def _():
        ends.wait_send()

    couple.wait()


def run_exchange(y, *, colour, windows):
    columns = y.shape[1]
    anywhere = pl.BlockSpec(memory_space=pl.ANY)
    return pl.pallas_call(
        functools.partial(exchange, colour, windows),
        out_shape=jax.ShapeDtypeStruct((COUPLE + BOUND, columns), y.dtype),
        in_specs=[anywhere],
        out_specs=anywhere,
        scratch_shapes=[pltpu.SemaphoreType.DMA((2,)), pltpu.SemaphoreType.DMA((2,))],
        compiler_params=pltpu.CompilerParams(
            collective_id=colour, has_side_effects=True, vmem_limit_bytes=1024 * 1024),
        name="exchange_%d" % colour,
    )(y)


def settle_all(scalars, bounds, t_in, inbox, limits, mail, has_before, settle):
    start_row = COUPLE + BOUND
    size = t_in.shape[0]
    half_link = 0.5 * scalars[1].astype(jnp.float32)

    def clipped_part(i):
        rows = pl.ds(pl.multiple_of(i * PART, PART), PART)
        t = t_in[rows, :]
        return rows, t, clipped(bounds, rows, t)

    def alone(i, _):
        rows, t, y = clipped_part(i)
        settle(rows, i, t, y)
        return _

    def starting(i, _):
        rows, t, y = clipped_part(start_row // PART + i)
        before = inbox[pl.ds(pl.multiple_of(COUPLE + i * PART, PART), PART), :]
        settle(rows, start_row // PART + i, t, 0.5 * (y + jnp.where(has_before, before, 0.0)))
        return _

    def coupled(i, _):
        rows, t, y = clipped_part(i)
        settle(rows, i, t, y + half_link * (inbox[rows, :] - y))
        return _

    limits.wait()
    lax.fori_loop(COUPLE // PART, start_row // PART, alone, 0)
    lax.fori_loop((start_row + BOUND) // PART, size // PART, alone, 0)
    mail.wait()
    lax.fori_loop(0, BOUND // PART, starting, 0)
    lax.fori_loop(0, COUPLE // PART, coupled, 0)


def clipped(bounds, rows, t):
    return jnp.minimum(jnp.maximum(t, bounds[rows, 0:1]), bounds[rows, 1:2])


def update(scalars, partners, adjacency, kkt, costs_in, bounds_in, t_in, inbox_in,
           t_out, y_out, next_scalars, colour, kk, costs, bounds, inbox, v, load_kkt, load_costs, load):
    area = lax.axis_index("area")
    win = lax.axis_index("win")
    tiles = kk.shape[0] // TILE
    limits = pltpu.make_async_copy(bounds_in, bounds, load.at[0])
    mail = pltpu.make_async_copy(inbox_in, inbox, load.at[1])
    limits.start()
    mail.start()

    def part_of_costs(i):
        rows = pl.ds(pl.multiple_of(i * PART, PART), PART)
        return pltpu.make_async_copy(costs_in.at[rows], costs.at[rows], load_costs.at[i])

    for i in range(tiles * TILE // PART):
        part_of_costs((i + COUPLE // PART) % (tiles * TILE // PART)).start()

    def part_of_kkt(i):
        rows = pl.ds(pl.multiple_of(i * PART, PART), PART)
        return pltpu.make_async_copy(kkt.at[rows], kk.at[rows], load_kkt.at[i])

    for i in range(tiles * TILE // PART):
        part_of_kkt(i).start()

    now = scalars[0]
    next_scalars[0] = now + 1
    next_scalars[1] = jnp.where(adjacency[area, partners[now, area]] == 1, 1, 0)
    colour[0] = partners[now, 0] - 1

    def settle(rows, part, t, z):
        u = t - z
        t_out[rows, :] = u
        part_of_costs(part).wait()
        v[rows, :] = (costs[rows, :] + z - u).astype(v.dtype)

    settle_all(scalars, bounds, t_in, inbox, limits, mail, jnp.logical_and(win > 0, now > 0), settle)

    def solve(i, _):
        rows = pl.ds(pl.multiple_of(i * TILE, TILE), TILE)
        for j in range(TILE // PART):
            part_of_kkt(i * (TILE // PART) + j).wait()

        t = jnp.dot(kk[rows, :], v[...], preferred_element_type=jnp.float32) + t_out[rows, :]
        t_out[rows, :] = t

        @pl.when(i < y_out.shape[0] // TILE)
        def _():
            y_out[rows, :] = clipped(bounds, rows, t)

        return 0

    lax.fori_loop(0, tiles, solve, 0)


def finish(scalars, bounds_in, t_in, inbox_in, z_out, u_out, bounds, inbox, z_kept, u_kept, load, done):
    limits = pltpu.make_async_copy(bounds_in, bounds, load.at[0])
    mail = pltpu.make_async_copy(inbox_in, inbox, load.at[1])
    limits.start()
    mail.start()

    def leaving(part):
        rows = pl.ds(pl.multiple_of(part * PART, PART), PART)
        return (pltpu.make_async_copy(z_kept.at[rows], z_out.at[rows], done.at[0, part]),
                pltpu.make_async_copy(u_kept.at[rows], u_out.at[rows], done.at[1, part]))

    def settle(rows, part, t, z):
        z_kept[rows, :] = z
        u_kept[rows, :] = t - z
        for copy in leaving(part):
            copy.start()

    settle_all(scalars, bounds, t_in, inbox, limits, mail, lax.axis_index("win") > 0, settle)

    def gone(part, _):
        for copy in leaving(part):
            copy.wait()
        return _

    lax.fori_loop(0, t_in.shape[0] // PART, gone, 0)


def run_finish(scalars, bounds, t, inbox):
    inside = pl.BlockSpec(memory_space=pltpu.VMEM)
    anywhere = pl.BlockSpec(memory_space=pl.ANY)
    like = jax.ShapeDtypeStruct(t.shape, t.dtype)
    return pl.pallas_call(
        finish,
        out_shape=(like, like),
        in_specs=[pl.BlockSpec(memory_space=pltpu.SMEM), anywhere, inside, anywhere],
        out_specs=(anywhere, anywhere),
        scratch_shapes=[
            pltpu.VMEM(bounds.shape, bounds.dtype),
            pltpu.VMEM(inbox.shape, inbox.dtype),
            pltpu.VMEM(t.shape, t.dtype),
            pltpu.VMEM(t.shape, t.dtype),
            pltpu.SemaphoreType.DMA((2,)),
            pltpu.SemaphoreType.DMA((2, t.shape[0] // PART)),
        ],
        compiler_params=pltpu.CompilerParams(vmem_limit_bytes=16 * 1024 * 1024),
        name="finish",
    )(scalars, bounds, t, inbox)


def run_update(scalars, partners, adjacency, kkt, costs, bounds, t, inbox):
    size, columns = costs.shape
    number = pl.BlockSpec(memory_space=pltpu.SMEM)
    inside = pl.BlockSpec(memory_space=pltpu.VMEM)
    anywhere = pl.BlockSpec(memory_space=pl.ANY)
    return pl.pallas_call(
        update,
        out_shape=(
            jax.ShapeDtypeStruct(t.shape, t.dtype),
            jax.ShapeDtypeStruct((COUPLE + BOUND, columns), t.dtype),
            jax.ShapeDtypeStruct(scalars.shape, scalars.dtype),
            jax.ShapeDtypeStruct((1,), jnp.int32),
        ),
        in_specs=[number] * 3 + [anywhere, anywhere, anywhere, inside, anywhere],
        out_specs=(inside, inside, number, number),
        scratch_shapes=[
            pltpu.VMEM(kkt.shape, kkt.dtype),
            pltpu.VMEM(costs.shape, costs.dtype),
            pltpu.VMEM(bounds.shape, bounds.dtype),
            pltpu.VMEM(inbox.shape, inbox.dtype),
            pltpu.VMEM((size, columns), jnp.bfloat16),
            pltpu.SemaphoreType.DMA((size // PART,)),
            pltpu.SemaphoreType.DMA((size // PART,)),
            pltpu.SemaphoreType.DMA((2,)),
        ],
        input_output_aliases={6: 0},
        compiler_params=pltpu.CompilerParams(vmem_limit_bytes=24 * 1024 * 1024),
        cost_estimate=pl.CostEstimate(
            flops=2 * size * size * columns, bytes_accessed=2 * size * size, transcendentals=0),
        name="update",
    )(scalars, partners, adjacency, kkt, costs, bounds, t, inbox)


def local(kkt, offsets, lower, upper, partners, adjacency):
    costs = offsets[0, 0]
    matrix = kkt[0, 0]
    bounds = jnp.stack([lower[0, 0], upper[0, 0]], axis=1)
    count = lax.axis_size("area")
    windows = lax.axis_size("win")
    branches = [functools.partial(run_exchange, colour=c, windows=windows) for c in range(1, count)]

    def iterate(_, state):
        t, inbox, scalars = state
        t, y, scalars, colour = run_update(scalars, partners, adjacency, matrix, costs, bounds, t, inbox)
        inbox = lax.switch(colour[0], branches, y)
        return t, inbox, scalars

    t, inbox, scalars = lax.fori_loop(0, ITERS, iterate, (
        jnp.zeros_like(costs), jnp.zeros((COUPLE + BOUND, costs.shape[1]), costs.dtype), jnp.zeros((2,), jnp.int32)))
    z, u = run_finish(scalars, bounds, t, inbox)
    return (z[None, None], u[None, None])


def solution(mesh):
    in_specs = (
        P("area", "win", None, None),
        P("area", "win", None, None),
        P("area", "win", None),
        P("area", "win", None),
        P(),
        P(),
    )
    out_specs = (P("area", "win", None, None), P("area", "win", None, None))
    return jax.shard_map(local, mesh=mesh, in_specs=in_specs, out_specs=out_specs, check_vma=False)
```
